256 devices in a mesh: fsdp: 64 (over y, x, z_hi), sp: 4 (over z_lo, core).
Axes of the slice: x: 4, y: 4, z: 8 (z_hi: 4, z_lo: 2; z = z_hi * 2 + z_lo), core: 2. Of those that a mesh axis runs over, the one named last changes fastest.
Arguments:
- gate_pre: bfloat16 [16384, 14848], P('fsdp', 'sp'), may hold values from -6 to 6
- up_pre: bfloat16 [16384, 14848], P('fsdp', 'sp'), may hold values from -6 to 6
- target_rows: bfloat16 [16384, 4096], P('fsdp'), may hold values from -6 to 6
- down_weight: bfloat16 [14848, 4096], P('sp', 'fsdp'), may hold values from -0.046875 to 0.046875
- old_logp: float32 [16384], P('fsdp'), may hold values from -3 to 3
- advantages: float32 [128], P('fsdp'), may hold values from -4 to 4
- lengths: int32 [128], P('fsdp'), may hold values from 32 to 112, as said below
- handoff: int32 [64], P('fsdp'), may hold values from 0 to 32, as said below
Outputs:
- gate_grad: bfloat16 [16384, 14848], P('fsdp', 'sp')
- up_grad: bfloat16 [16384, 14848], P('fsdp', 'sp')
- loss: float32 [], replicated
The draws below stay inside these ranges and needn't reach their ends.
Inputs may be any that keep to these rules, and one draw needn't show every extreme that they name: `lengths`: two responses per index of fsdp, stored one after the other from the first of its 256 rows; the rows after them are padding. The first response has exactly 112 tokens. Index g of fsdp hands the last handoff[g] rows of its second response to index g + 1. The last index hands on nothing; index 0 and the next-to-last index hand on exactly 32.
All inputs are finite; a program needn't handle non-finite values.
Results may differ from the reference program's by a relative error of at most 0.0024.
Values may be sent and summed in bfloat16 or wider, within the bound.
No kernel may reach another device: no remote copies, remote signals or barrier semaphores. Data moves between devices by JAX's collectives and lax.ppermute only.
A program may use at most 128 MiB of HBM per device.

```python
import jax
import jax.numpy as jnp
from jax import lax

D = 4096
FF = 14848
TOK_DEV = 256
TOKENS = 16384
RESP = 128
SPARE = 32
N_FSDP = 64


def draw_lengths(key, part):
    key = jax.random.fold_in(key, 7)
    longest = TOK_DEV // 2 - TOK_DEV // 16
    sampled = jax.random.randint(key, (RESP,), TOK_DEV // 8, longest + 1, dtype=jnp.int32)
    return sampled.at[0].set(longest)


def draw_handoff(key, part):
    key = jax.random.fold_in(key, 11)
    sampled = jax.random.randint(key, (N_FSDP,), 0, SPARE + 1, dtype=jnp.int32)
    return sampled.at[0].set(SPARE).at[N_FSDP - 2].set(SPARE).at[N_FSDP - 1].set(0)


def shard_levels(own_key, shape, split, low, top_value):
    def one(axis_at, blocks):
        steps = jax.random.uniform(jax.random.fold_in(jax.random.fold_in(own_key, 6), axis_at), (blocks,), jnp.float32, low / len(split), top_value / len(split))
        return jnp.repeat(jnp.exp(steps), shape[axis_at] // blocks).reshape((-1,) + (1,) * (len(shape) - axis_at - 1))

    gain = one(*split[0])
    for cut in split[1:]:
        gain = gain * one(*cut)
    return gain


def centred(rng, shape, deviation, bound, pieces=(), held_as=jnp.bfloat16):
    result = deviation * jax.random.normal(rng, shape, jnp.float32)
    if pieces:
        result = result * shard_levels(rng, shape, pieces, -0.22, 0.18)
    return jnp.clip(result, -bound, bound).astype(held_as)


def setup_inputs(seed: int = 0) -> dict:
    keys = jax.random.split(jax.random.key(seed), 9)
    return {
        "gate_pre": centred(keys[0], (TOKENS, FF), 1.0, 6.0, ((0, 64), (1, 4))),
        "up_pre": centred(keys[1], (TOKENS, FF), 1.0, 6.0, ((0, 64), (1, 4))),
        "target_rows": centred(keys[2], (TOKENS, D), 1.0, 6.0, ((0, 64),)),
        "down_weight": centred(keys[3], (FF, D), FF ** -0.5, 0.046875, ((0, 4), (1, 64))),
        "old_logp": centred(keys[4], (TOKENS,), 0.5, 3.0, ((0, 64),), jnp.float32),
        "advantages": centred(keys[5], (RESP,), 1.0, 4.0, ((0, 64),), jnp.float32),
        "lengths": draw_lengths(jax.random.fold_in(keys[8], 71), 0),
        "handoff": draw_handoff(jax.random.fold_in(keys[8], 71), 0),
    }


def per_replica(inputs, down_weight, token_count):
    gate_in, up_in, target_in, old_in, pair_len, pair_adv = inputs
    inv_root = 1.0 / (D ** 0.5)
    probe_rows = jnp.dot(target_in, down_weight.T, preferred_element_type=jnp.float32) * inv_root
    gate_float = gate_in.astype(jnp.float32)
    up_float = up_in.astype(jnp.float32)
    sigmoid_gate = jax.nn.sigmoid(gate_float)
    activated = gate_float * sigmoid_gate
    token_score = jnp.sum(activated * up_float * probe_rows, axis=1)
    positions = jnp.arange(TOK_DEV, dtype=jnp.int32)
    in_first = positions < pair_len[0]
    in_second = jnp.logical_and(positions >= pair_len[0], positions < pair_len[0] + pair_len[1])
    live_mask = jnp.logical_or(in_first, in_second).astype(jnp.float32)
    row_adv = (jnp.where(in_first, pair_adv[0], 0.0) + jnp.where(in_second, pair_adv[1], 0.0)).astype(jnp.float32)
    prob_ratio = jnp.exp(token_score - old_in)
    plain_term = prob_ratio * row_adv
    clipped_term = jnp.clip(prob_ratio, 0.8, 1.2) * row_adv
    loss_part = jnp.sum(live_mask * jnp.minimum(plain_term, clipped_term))
    slope_row = jnp.where(plain_term <= clipped_term, -row_adv * prob_ratio, 0.0) * live_mask
    dhidden = slope_row[:, None] * probe_rows / token_count
    home_gate = (dhidden * up_float * sigmoid_gate * (1.0 + gate_float * (1.0 - sigmoid_gate))).astype(jnp.bfloat16)
    home_up = (dhidden * activated).astype(jnp.bfloat16)
    return home_gate, home_up, loss_part


def take_tail(array, kept_rows):
    return lax.dynamic_slice_in_dim(array, kept_rows, SPARE, 0)


def place_tail(array, arrived, kept_rows):
    return lax.dynamic_update_slice_in_dim(array, arrived, kept_rows, 0)


def relay(home, kept):
    blocks = jax.vmap(take_tail)(home, kept)
    previous = jnp.concatenate([jnp.zeros((1, SPARE, FF), jnp.bfloat16), blocks[:-1]], axis=0)
    return jax.vmap(place_tail)(home, previous, kept).reshape(TOKENS, FF)


def reference(gate_pre, up_pre, target_rows, down_weight, old_logp, advantages, lengths, handoff):
    token_count = jnp.sum(lengths).astype(jnp.float32)
    length_pairs = lengths.reshape(N_FSDP, 2)
    adv_pairs = advantages.reshape(N_FSDP, 2)
    inputs = (gate_pre.reshape(N_FSDP, TOK_DEV, FF), up_pre.reshape(N_FSDP, TOK_DEV, FF),
              target_rows.reshape(N_FSDP, TOK_DEV, D), old_logp.reshape(N_FSDP, TOK_DEV),
              length_pairs, adv_pairs)
    home_gate, home_up, loss_parts = lax.map(lambda item: per_replica(item, down_weight, token_count), inputs)
    kept = (length_pairs[:, 0] + length_pairs[:, 1] - handoff).astype(jnp.int32)
    gate_grad = relay(home_gate, kept)
    up_grad = relay(home_up, kept)
    loss_value = -jnp.sum(loss_parts) / token_count
    return gate_grad, up_grad, loss_value
```

```python
import functools

import jax
import jax.numpy as jnp
from jax import lax
from jax.experimental import pallas as pl
from jax.experimental.pallas import tpu as pltpu
from jax.sharding import Mesh, PartitionSpec as P

D = 4096
ROWS = 256
SPARE = 32
MINE = 3712
LANES = 128
STEP = 896
CHUNK = 1024
STAGES = 2
WIDE = CHUNK // STAGES
FS = ("y", "x", "h")
MIB = 1024 * 1024


def shift(value, axis, by):
    return lax.ppermute(value, axis, [(i, (i + by) % 4) for i in range(4)])


def mix(value, axis, bit):
    n = lax.axis_size(axis)
    return lax.ppermute(value, axis, [(i, i ^ bit) for i in range(n)])


def total(value):
    for axis in ("h", "x", "y"):
        value = (value + mix(value, axis, 1)) + (mix(value, axis, 2) + mix(value, axis, 3))
    return value


def relayed(array, kept, axis):
    tail = lax.dynamic_slice_in_dim(array, kept, SPARE, axis)
    tail = lax.ppermute(tail, FS, [(i, i + 1) for i in range(63)])
    return lax.dynamic_update_slice_in_dim(array, tail, kept, axis)


def ring(block, axis, forward):
    after = shift(block, axis, 1)
    before = shift(block, axis, -1)
    far = shift(after, axis, 1) if forward else shift(before, axis, -1)
    return [block, after, far, before]


def probe_kernel(pos, rows_ref, *refs):
    pieces, (out_ref, weight, sems) = refs[:16], refs[16:]

    @pl.when(pl.program_id(0) == 0)
    def _():
        copies = []
        for dy in range(4):
            for dh in range(4):
                k = dy * 4 + dh
                y = lax.rem(pos[1] + 4 - dy, 4)
                h = lax.rem(pos[2] + 4 - dh, 4)
                copy = pltpu.make_async_copy(pieces[k], weight.at[y, :, h], sems.at[k])
                copy.start()
                copies.append(copy)
        for copy in copies:
            copy.wait()

    product = jnp.dot(
        rows_ref[...], weight[...].reshape(D, WIDE), preferred_element_type=jnp.float32
    )
    out_ref[0] = product * (1.0 / D**0.5)


def probes(pos, rows, pieces):
    return pl.pallas_call(
        probe_kernel,
        grid_spec=pltpu.PrefetchScalarGridSpec(
            num_scalar_prefetch=1,
            grid=(4,),
            in_specs=[pl.BlockSpec((ROWS, D), lambda r, pos: (lax.rem(pos[0] + r, 4), 0))]
            + [pl.BlockSpec(memory_space=pl.ANY)] * 16,
            out_specs=pl.BlockSpec((1, ROWS, WIDE), lambda r, pos: (r, 0, 0)),
            scratch_shapes=[
                pltpu.VMEM((4, 4, 4, 64, WIDE), jnp.bfloat16),
                pltpu.SemaphoreType.DMA((16,)),
            ],
        ),
        out_shape=jax.ShapeDtypeStruct((4, ROWS, WIDE), jnp.float32),
        compiler_params=pltpu.CompilerParams(vmem_limit_bytes=48 * MIB),
        cost_estimate=pl.CostEstimate(
            flops=2 * 1024 * D * WIDE, bytes_accessed=2 * D * (1024 + WIDE), transcendentals=0
        ),
        name="probe",
    )(pos, rows, *pieces)


def tiles(pos):
    for k in range(4):
        member = lax.rem(pos[0] + 4 - k, 4)
        for s in range(STAGES):
            for t in range(WIDE // LANES):
                place = member * STEP + (s * WIDE + t * LANES)
                last = s == STAGES - 1 and t == WIDE // LANES - 1
                yield k * STAGES + s, t, pl.multiple_of(place, LANES), member, last


def part(ref, t):
    return ref[0, :, t * LANES : (t + 1) * LANES]


def score_kernel(pos, gate_ref, up_ref, *refs):
    pieces, out_ref = refs[:-1], refs[-1]
    acc = jnp.zeros((LANES, LANES), jnp.float32)
    for k, t, place, member, last in tiles(pos):
        gate = gate_ref[:, pl.ds(place, LANES)].astype(jnp.float32)
        up = up_ref[:, pl.ds(place, LANES)].astype(jnp.float32)
        term = gate * jax.nn.sigmoid(gate) * up * part(pieces[k], t)
        if last:
            term = jnp.where(member == 3, term, 0.0)
        acc = acc + term
    out_ref[0] = jnp.sum(acc.T, axis=0, keepdims=True)


def piece_specs(rows):
    return [pl.BlockSpec((1, rows, WIDE), lambda i, pos: (0, i, 0))] * (4 * STAGES)


def scores(pos, gate, up, pieces):
    wide = pl.BlockSpec((LANES, MINE), lambda i, pos: (i, 0))
    return pl.pallas_call(
        score_kernel,
        grid_spec=pltpu.PrefetchScalarGridSpec(
            num_scalar_prefetch=1,
            grid=(2,),
            in_specs=[wide, wide] + piece_specs(LANES),
            out_specs=pl.BlockSpec((1, 1, LANES), lambda i, pos: (i, 0, 0)),
        ),
        out_shape=jax.ShapeDtypeStruct((2, 1, LANES), jnp.float32),
        compiler_params=pltpu.CompilerParams(vmem_limit_bytes=48 * MIB),
        cost_estimate=pl.CostEstimate(
            flops=8 * ROWS * MINE, bytes_accessed=8 * ROWS * MINE, transcendentals=ROWS * MINE
        ),
        name="score",
    )(pos, gate, up, *pieces)


def slope_kernel(score_ref, info_ref, count_ref, slope_ref, loss_ref):
    loss = jnp.zeros((1, LANES), jnp.float32)
    for i in range(2):
        old = info_ref[0, i]
        adv = info_ref[1, i]
        mask = info_ref[2, i]
        ratio = jnp.exp(score_ref[i] - old)
        plain = ratio * adv
        clipped = jnp.clip(ratio, 0.8, 1.2) * adv
        loss = loss + mask * jnp.minimum(plain, clipped)
        slope = jnp.where(plain <= clipped, -adv * ratio, 0.0) * mask / count_ref[...]
        slope_ref[i * LANES : (i + 1) * LANES, :] = jnp.broadcast_to(slope, (LANES, LANES)).T
    loss_ref[...] = loss


def slopes(score, info, count):
    return pl.pallas_call(
        slope_kernel,
        out_shape=(
            jax.ShapeDtypeStruct((ROWS, LANES), jnp.float32),
            jax.ShapeDtypeStruct((1, LANES), jnp.float32),
        ),
        name="slope",
    )(score, info, count)


def grad_kernel(pos, gate_ref, up_ref, slope_ref, *refs):
    pieces, (gate_out, up_out) = refs[:-2], refs[-2:]
    slope = slope_ref[...]
    for k, t, place, _, _ in tiles(pos):
        here = pl.ds(place, LANES)
        gate = gate_ref[:, here].astype(jnp.float32)
        up = up_ref[:, here].astype(jnp.float32)
        sig = jax.nn.sigmoid(gate)
        dhidden = slope * part(pieces[k], t)
        gate_out[:, here] = (dhidden * up * sig * (1.0 + gate * (1.0 - sig))).astype(jnp.bfloat16)
        up_out[:, here] = (dhidden * (gate * sig)).astype(jnp.bfloat16)


def grads(pos, gate, up, slope, pieces):
    rows = 64
    wide = pl.BlockSpec((rows, MINE), lambda i, pos: (i, 0))
    return pl.pallas_call(
        grad_kernel,
        grid_spec=pltpu.PrefetchScalarGridSpec(
            num_scalar_prefetch=1,
            grid=(ROWS // rows,),
            in_specs=[wide, wide, pl.BlockSpec((rows, LANES), lambda i, pos: (i, 0))]
            + piece_specs(rows),
            out_specs=[wide, wide],
        ),
        out_shape=[jax.ShapeDtypeStruct((ROWS, MINE), jnp.bfloat16)] * 2,
        compiler_params=pltpu.CompilerParams(vmem_limit_bytes=48 * MIB),
        cost_estimate=pl.CostEstimate(
            flops=12 * ROWS * MINE, bytes_accessed=12 * ROWS * MINE, transcendentals=ROWS * MINE
        ),
        name="grad",
    )(pos, gate, up, slope, *pieces)


def shards(gate_pre, up_pre, target_rows, down_weight, old_logp, advantages, lengths, handoff):
    my_x = lax.axis_index("x")
    pos = jnp.stack([my_x, lax.axis_index("y"), lax.axis_index("h")]).astype(jnp.int32)
    kept = lengths[0] + lengths[1] - handoff[0]

    columns = down_weight.T
    sent = []
    for by in range(4):
        start = lax.rem(my_x + by, 4) * STEP
        chunk = lax.dynamic_slice_in_dim(columns, start, CHUNK, 1)
        sent.append(chunk if by == 0 else shift(chunk, "x", by))
    order = [lax.rem(my_x + 4 - x, 4) for x in range(4)]
    mine = jnp.stack([lax.select_n(k, *sent) for k in order])
    pieces = []
    for s in range(STAGES):
        block = mine[:, :, s * WIDE : (s + 1) * WIDE]
        near = ring(block, "h", s % 2 == 0)
        whole = [ring(b, "y", dh < 2) for dh, b in enumerate(near)]
        pieces.append([whole[dh][dy] for dy in range(4) for dh in range(4)])

    rows = relayed(target_rows, kept, 0)
    half = lax.dynamic_slice_in_dim(rows, lax.axis_index("c") * LANES, LANES, 0)
    group = lax.all_gather(half, ("x", "c"), axis=0, tiled=True)
    positions = jnp.arange(ROWS, dtype=jnp.int32)
    in_first = positions < lengths[0]
    in_second = jnp.logical_and(positions >= lengths[0], positions < lengths[0] + lengths[1])
    live = jnp.logical_or(in_first, in_second).astype(jnp.float32)
    adv = jnp.where(in_first, advantages[0], 0.0) + jnp.where(in_second, advantages[1], 0.0)
    info = relayed(jnp.stack([old_logp, adv, live]), kept, 1).reshape(3, 2, 1, LANES)
    gate = relayed(gate_pre, kept, 0)
    up = relayed(up_pre, kept, 0)
    count = total(jnp.full((1, LANES), jnp.sum(lengths).astype(jnp.float32)))

    home = [None] * (4 * STAGES)
    for s in range(STAGES):
        product = probes(pos, group, pieces[s])
        home[s] = product
        for by in range(1, 4):
            home[by * STAGES + s] = shift(product[by : by + 1], "x", by)
    partial = scores(pos, gate, up, home)
    score = partial + mix(partial, "c", 1)
    score = score + mix(score, "l", 1)
    slope, loss_part = slopes(score, info, count)
    gate_grad, up_grad = grads(pos, gate, up, slope, home)
    loss_sum = jnp.sum(total(loss_part))
    return gate_grad, up_grad, -loss_sum / count[0, 0]


def solution(mesh):
    grid = Mesh(mesh.devices.reshape(4, 4, 4, 2, 2), ("y", "x", "h", "l", "c"))
    sp = ("l", "c")
    return jax.shard_map(
        shards,
        mesh=grid,
        in_specs=(P(FS, sp), P(FS, sp), P(FS, None), P(sp, FS), P(FS), P(FS), P(FS), P(FS)),
        out_specs=(P(FS, sp), P(FS, sp), P()),
        check_vma=False,
    )
```

```python
import functools

import jax
import jax.numpy as jnp
from jax import lax
from jax.experimental import pallas as pl
from jax.experimental.pallas import tpu as pltpu
from jax.sharding import Mesh, PartitionSpec as P

D = 4096
ROWS = 256
SPARE = 32
MINE = 3712
LANES = 128
STEP = 896
CHUNK = 1024
FS = ("y", "x", "h")
CUTS = ((0, 512), (512, 512))
OWN, SIDE, OTHER, FAR = range(4)
MIB = 1024 * 1024


def swing(value, axis, way):
    pairs = []
    for i in range(4):
        for c in range(2):
            to = (i + {SIDE: 1 + 2 * c, OTHER: 3 + 2 * c, FAR: 2}[way]) % 4
            pairs.append((i * 2 + c, to * 2 + c))
    return lax.ppermute(value, (axis, "c"), pairs)


def mix(value, axis, bit):
    n = lax.axis_size(axis)
    return lax.ppermute(value, axis, [(i, i ^ bit) for i in range(n)])


def spread(value, axis):
    return (value + mix(value, axis, 1)) + (mix(value, axis, 2) + mix(value, axis, 3))


def tie(*values):
    return lax.optimization_barrier(values)


def onward(tail):
    return lax.ppermute(tail, FS, [(i, i + 1) for i in range(63)])


def moved(kept, own, tail):
    first = jnp.minimum(kept // 16 * 16, ROWS - 48)
    offset = kept - first
    window = pl.ds(pl.multiple_of(first, 16), 48)
    row = lax.broadcasted_iota(jnp.int32, (48, SPARE), 0)
    column = lax.broadcasted_iota(jnp.int32, (48, SPARE), 1)
    pick = (row == column + offset).astype(jnp.bfloat16)
    row = lax.broadcasted_iota(jnp.int32, (48, tail.shape[1]), 0)
    fresh = jnp.logical_and(row >= offset, row < offset + SPARE)
    new = jnp.dot(pick, tail, preferred_element_type=jnp.float32)
    return window, jnp.where(fresh, new, own[window, :].astype(jnp.float32)).astype(jnp.bfloat16)


def rows_kernel(where, own, tail, out_ref):
    out_ref[...] = own[...]
    window, new = moved(where[0], own, tail[...])
    out_ref[window, :] = new


def half_rows(where, rows, tail):
    return pl.pallas_call(
        rows_kernel,
        grid_spec=pltpu.PrefetchScalarGridSpec(
            num_scalar_prefetch=1,
            grid=(1,),
            in_specs=[
                pl.BlockSpec((ROWS, 2048), lambda i, where: (0, where[1])),
                pl.BlockSpec((SPARE, 2048), lambda i, where: (0, 0)),
            ],
            out_specs=pl.BlockSpec((ROWS, 2048), lambda i, where: (0, 0)),
        ),
        out_shape=jax.ShapeDtypeStruct((ROWS, 2048), jnp.bfloat16),
        compiler_params=pltpu.CompilerParams(vmem_limit_bytes=32 * MIB),
        name="rows",
    )(where, rows, tail)


def place_kernel(kept, gate, up, tails, gate_out, up_out):
    for own, tail, out in ((gate, tails[0], gate_out), (up, tails[1], up_out)):
        out[...] = own[...]
        window, new = moved(kept[0], own, tail)
        out[window, :] = new


def placed(kept, gate, up, tails):
    vmem = pl.BlockSpec(memory_space=pltpu.VMEM)
    return pl.pallas_call(
        place_kernel,
        in_specs=[pl.BlockSpec(memory_space=pltpu.SMEM)] + [vmem] * 3,
        out_specs=[vmem] * 2,
        out_shape=[jax.ShapeDtypeStruct((ROWS, MINE), jnp.bfloat16)] * 2,
        compiler_params=pltpu.CompilerParams(vmem_limit_bytes=60 * MIB),
        cost_estimate=pl.CostEstimate(flops=0, bytes_accessed=8 * ROWS * MINE, transcendentals=0),
        name="place",
    )(kept, gate, up, tails)


def start_all(pairs, sems):
    copies = [pltpu.make_async_copy(a, b, sems.at[k]) for k, (a, b) in enumerate(pairs)]
    for copy in copies:
        copy.start()
    return copies


def wait_all(copies):
    for copy in copies:
        copy.wait()


def probe_kernel(pos, rows_ref, *refs):
    parts, outs, (weight, rows, sems) = refs[:4], refs[4:8], refs[8:]
    waits = []
    for ky in range(4):
        half = pos[ky] // 2
        lanes = pl.ds(pl.multiple_of(lax.rem(pos[ky], 2) * 1024, 1024), 1024)
        pairs = [(parts[ky].at[k], weight.at[ky, :, pos[8 + k]]) for k in range(4)]
        for k in range(4):
            to = rows.at[ky, pl.ds(k * ROWS, ROWS)]
            pairs.append((rows_ref.at[pos[4 + k] * 2 + half, :, lanes], to))
        waits.append(start_all(pairs, sems.at[ky]))
    for ky in range(4):
        wait_all(waits[ky])
        product = jnp.dot(
            rows[ky], weight[ky].reshape(1024, -1), preferred_element_type=jnp.float32
        )
        for k in range(4):
            value = product[k * ROWS : (k + 1) * ROWS] * (1.0 / D**0.5)
            outs[k][...] = value if ky == 0 else outs[k][...] + value


def probes(pos, rows, parts):
    wide = parts[0].shape[-1]
    vmem = pl.BlockSpec(memory_space=pltpu.VMEM)
    return pl.pallas_call(
        probe_kernel,
        in_specs=[pl.BlockSpec(memory_space=pltpu.SMEM)] + [pl.BlockSpec(memory_space=pl.ANY)] * 5,
        out_specs=[vmem] * 4,
        scratch_shapes=[
            pltpu.VMEM((4, 4, 4, 64, wide), jnp.bfloat16),
            pltpu.VMEM((4, 4 * ROWS, 1024), jnp.bfloat16),
            pltpu.SemaphoreType.DMA((4, 8)),
        ],
        out_shape=[jax.ShapeDtypeStruct((ROWS, wide), jnp.float32)] * 4,
        compiler_params=pltpu.CompilerParams(vmem_limit_bytes=60 * MIB),
        cost_estimate=pl.CostEstimate(
            flops=8 * ROWS * D * wide, bytes_accessed=2 * D * (1024 + wide), transcendentals=0
        ),
        name="probe",
    )(pos, rows, *parts)


def tiles(pos):
    for k in range(4):
        member = pos[4 + k]
        for t in range(CHUNK // LANES):
            cut = max(i for i, (first, _) in enumerate(CUTS) if first <= t * LANES)
            there = t * LANES - CUTS[cut][0]
            place = pl.multiple_of(member * STEP + t * LANES, LANES)
            yield 4 * cut + k, slice(there, there + LANES), pl.ds(place, LANES), t, member


def score_kernel(pos, gate_ref, up_ref, *refs):
    pieces, out_ref = refs[:-1], refs[-1]
    acc = jnp.zeros((LANES, LANES), jnp.float32)
    for k, there, here, t, member in tiles(pos):
        gate = gate_ref[:, here].astype(jnp.float32)
        up = up_ref[:, here].astype(jnp.float32)
        term = gate * jax.nn.sigmoid(gate) * up * pieces[k][:, there]
        if t == CHUNK // LANES - 1:
            term = jnp.where(member == 3, term, 0.0)
        acc = acc + term
    out_ref[0] = jnp.sum(acc.T, axis=0, keepdims=True)


def piece_specs(rows):
    return [pl.BlockSpec((rows, n), lambda i, pos: (i, 0)) for _, n in CUTS for _ in range(4)]


def scores(pos, gate, up, pieces):
    wide = pl.BlockSpec((LANES, MINE), lambda i, pos: (i, 0))
    return pl.pallas_call(
        score_kernel,
        grid_spec=pltpu.PrefetchScalarGridSpec(
            num_scalar_prefetch=1,
            grid=(2,),
            in_specs=[wide, wide] + piece_specs(LANES),
            out_specs=pl.BlockSpec((1, 1, LANES), lambda i, pos: (i, 0, 0)),
        ),
        out_shape=jax.ShapeDtypeStruct((2, 1, LANES), jnp.float32),
        compiler_params=pltpu.CompilerParams(vmem_limit_bytes=60 * MIB),
        cost_estimate=pl.CostEstimate(
            flops=8 * ROWS * MINE, bytes_accessed=8 * ROWS * MINE, transcendentals=ROWS * MINE
        ),
        name="score",
    )(pos, gate, up, *pieces)


def info_kernel(nums, advs, old_ref, info_ref, tail_ref):
    at = lax.broadcasted_iota(jnp.int32, (1, ROWS), 1)
    in_first = at < nums[0]
    in_second = jnp.logical_and(at >= nums[0], at < nums[0] + nums[1])
    adv = jnp.where(in_first, advs[0], 0.0) + jnp.where(in_second, advs[1], 0.0)
    live = jnp.logical_or(in_first, in_second).astype(jnp.float32)
    row = lax.broadcasted_iota(jnp.int32, (8, ROWS), 0)
    info = jnp.where(row == 0, old_ref[...], jnp.where(row == 1, adv, live))
    info_ref[...] = info
    tail_ref[...] = pltpu.roll(info, ROWS - nums[2], 1)[:, :LANES]


def infos(nums, advs, old):
    smem = pl.BlockSpec(memory_space=pltpu.SMEM)
    return pl.pallas_call(
        info_kernel,
        in_specs=[smem, smem, pl.BlockSpec(memory_space=pltpu.VMEM)],
        out_shape=(
            jax.ShapeDtypeStruct((8, ROWS), jnp.float32),
            jax.ShapeDtypeStruct((8, LANES), jnp.float32),
        ),
        name="info",
    )(nums, advs, old)


def slope_kernel(nums, score_ref, info_ref, tail_ref, count_ref, slope_ref, loss_ref):
    at = lax.broadcasted_iota(jnp.int32, (8, ROWS), 1)
    fresh = jnp.logical_and(at >= nums[2], at < nums[2] + SPARE)
    tail = jnp.concatenate([tail_ref[...], tail_ref[...]], axis=1)
    info = jnp.where(fresh, pltpu.roll(tail, nums[2], 1), info_ref[...])
    loss = jnp.zeros((1, LANES), jnp.float32)
    for i in range(2):
        here = slice(i * LANES, (i + 1) * LANES)
        old, adv, mask = info[0:1, here], info[1:2, here], info[2:3, here]
        ratio = jnp.exp(score_ref[i] - old)
        plain = ratio * adv
        clipped = jnp.clip(ratio, 0.8, 1.2) * adv
        loss = loss + mask * jnp.minimum(plain, clipped)
        slope = jnp.where(plain <= clipped, -adv * ratio, 0.0) * mask / count_ref[...]
        slope_ref[here, :] = jnp.broadcast_to(slope, (LANES, LANES)).T
    loss_ref[...] = loss


def slopes(nums, score, info, tail, count):
    vmem = pl.BlockSpec(memory_space=pltpu.VMEM)
    return pl.pallas_call(
        slope_kernel,
        in_specs=[pl.BlockSpec(memory_space=pltpu.SMEM)] + [vmem] * 4,
        out_shape=(
            jax.ShapeDtypeStruct((ROWS, LANES), jnp.float32),
            jax.ShapeDtypeStruct((1, LANES), jnp.float32),
        ),
        name="slope",
    )(nums, score, info, tail, count)


def grad_kernel(pos, gate_ref, up_ref, slope_ref, *refs):
    pieces, (gate_out, up_out) = refs[:-2], refs[-2:]
    slope = slope_ref[...]
    for k, there, here, _, _ in tiles(pos):
        gate = gate_ref[:, here].astype(jnp.float32)
        up = up_ref[:, here].astype(jnp.float32)
        sig = jax.nn.sigmoid(gate)
        dhidden = slope * pieces[k][:, there]
        gate_out[:, here] = (dhidden * up * sig * (1.0 + gate * (1.0 - sig))).astype(jnp.bfloat16)
        up_out[:, here] = (dhidden * (gate * sig)).astype(jnp.bfloat16)


def grads(pos, gate, up, slope, pieces):
    rows = 64
    wide = pl.BlockSpec((rows, MINE), lambda i, pos: (i, 0))
    return pl.pallas_call(
        grad_kernel,
        grid_spec=pltpu.PrefetchScalarGridSpec(
            num_scalar_prefetch=1,
            grid=(ROWS // rows,),
            in_specs=[wide, wide, pl.BlockSpec((rows, LANES), lambda i, pos: (i, 0))]
            + piece_specs(rows),
            out_specs=[wide, wide],
        ),
        out_shape=[jax.ShapeDtypeStruct((ROWS, MINE), jnp.bfloat16)] * 2,
        compiler_params=pltpu.CompilerParams(vmem_limit_bytes=60 * MIB),
        cost_estimate=pl.CostEstimate(
            flops=12 * ROWS * MINE, bytes_accessed=12 * ROWS * MINE, transcendentals=ROWS * MINE
        ),
        name="grad",
    )(pos, gate, up, slope, *pieces)


def shards(gate_pre, up_pre, target_rows, down_weight, old_logp, advantages, lengths, handoff):
    at = {a: lax.axis_index(a) for a in ("y", "x", "h", "c")}
    ahead = [0, 1 + 2 * at["c"], 3 + 2 * at["c"], 2]
    behind = [0, 3 + 2 * at["c"], 1 + 2 * at["c"], 2]
    to_x = [lax.rem(at["x"] + k, 4) for k in ahead]
    from_x = [lax.rem(at["x"] + k, 4) for k in behind]
    kept = lengths[0] + lengths[1] - handoff[0]
    columns = down_weight.T
    chunks = [lax.dynamic_slice_in_dim(columns, x * STEP, CHUNK, 1) for x in to_x]
    chunks, target_rows, kept, lengths = tie(chunks, target_rows, kept, lengths)
    sent = [chunks[0]] + [swing(chunks[way], "x", way) for way in (SIDE, OTHER, FAR)]
    count = jnp.full((1, LANES), jnp.sum(lengths).astype(jnp.float32))
    tail = onward(lax.dynamic_slice(target_rows, (kept, at["c"] * 2048), (SPARE, 2048)))
    nums = jnp.stack([lengths[0], lengths[1], kept]).astype(jnp.int32)
    info, info_tail = infos(nums, advantages, old_logp.reshape(1, ROWS))
    info_tail = onward(info_tail)
    sent, lengths, kept, count, tail, info_tail = tie(
        sent, lengths, kept, count, tail, info_tail
    )
    mine = []
    for x in range(4):
        piece = sent[0]
        for k in (SIDE, OTHER, FAR):
            piece = jnp.where(from_x[k] == x, sent[k], piece)
        mine.append(piece)
    pos = [lax.rem(at["y"] + k, 4) for k in behind] + from_x
    pos = jnp.stack(pos + [lax.rem(at["h"] + k, 4) for k in behind]).astype(jnp.int32)

    block = jnp.stack(mine)
    block = [block[:, :, a : a + n] for a, n in CUTS]
    tails = jnp.stack([lax.dynamic_slice_in_dim(a, kept, SPARE, 0) for a in (gate_pre, up_pre)])

    def there(value, axis):
        return swing(value, axis, SIDE), swing(value, axis, OTHER)

    def again(side, axis):
        return swing(side, axis, SIDE)

    def returned(product):
        home = [product[OWN], None, None, None]
        for k, way in ((SIDE, OTHER), (OTHER, SIDE), (FAR, FAR)):
            home[way] = swing(product[k], "x", way)
        return home

    side, other = there(block[0], "h")
    side, other = tie(side, other)
    far = again(side, "h")
    where = jnp.stack([kept, at["c"]]).astype(jnp.int32)
    group = lax.all_gather(half_rows(where, target_rows, tail), ("x", "c"), axis=0)
    home, parts = [], None
    last = len(CUTS) - 1
    for i in range(last + 1):
        wide = jnp.stack([block[i], side, other, far])
        wide, block, parts, count = tie(wide, block, parts, count)
        a, b = there(wide, "y")
        if i < last:
            side, other = there(block[i + 1], "h")
        if i == 0:
            count = lax.psum(count, "x")
        product = probes(pos, group, parts) if i else None
        a, b, side, other, count, product, home, tails = tie(
            a, b, side, other, count, product, home, tails
        )
        if i:
            home = home + returned(product)
        c = again(a, "y")
        if i < last:
            far = again(side, "h")
        if i == last - 1:
            count = lax.psum(count, "h")
        parts = [wide, a, b, c]
    tails = onward(tails)
    product = probes(pos, group, parts)
    product, home, count, tails = tie(product, home, count, tails)
    home = home + returned(product)
    count = lax.psum(count, "y")
    gate, up = placed(kept.reshape(1).astype(jnp.int32), gate_pre, up_pre, tails)
    gate, up, count, home[-3], home[-2] = tie(gate, up, count, home[-3], home[-2])
    score = lax.psum(scores(pos, gate, up, home), ("l", "c"))
    slope, loss_part = slopes(nums, score, info, info_tail, count)
    loss_part = spread(loss_part, "h")
    gate_grad, up_grad = grads(pos, gate, up, slope, home)
    loss_part, gate_grad, up_grad = tie(loss_part, gate_grad, up_grad)
    loss_sum = jnp.sum(spread(spread(loss_part, "y"), "x"))
    return gate_grad, up_grad, -loss_sum / count[0, 0]


def solution(mesh):
    grid = Mesh(mesh.devices.reshape(4, 4, 4, 2, 2), ("y", "x", "h", "l", "c"))
    sp = ("l", "c")
    return jax.shard_map(
        shards,
        mesh=grid,
        in_specs=(P(FS, sp), P(FS, sp), P(FS, None), P(sp, FS), P(FS), P(FS), P(FS), P(FS)),
        out_specs=(P(FS, sp), P(FS, sp), P()),
        check_vma=False,
    )
```

```python
import functools

import jax
import jax.numpy as jnp
from jax import lax
from jax.experimental import pallas as pl
from jax.experimental.pallas import tpu as pltpu
from jax.sharding import Mesh, PartitionSpec as P

D = 4096
ROWS = 256
SPARE = 32
MINE = 3712
LANES = 128
STEP = 896
CHUNK = 1024
FS = ("y", "x", "h")
CUTS = ((0, 512), (512, 512))
OWN, SIDE, OTHER, FAR = range(4)
MIB = 1024 * 1024


def swing(value, axis, way):
    pairs = []
    for i in range(4):
        for c in range(2):
            to = (i + {SIDE: 1 + 2 * c, OTHER: 3 + 2 * c, FAR: 2}[way]) % 4
            pairs.append((i * 2 + c, to * 2 + c))
    return lax.ppermute(value, (axis, "c"), pairs)


def mix(value, axis, bit):
    n = lax.axis_size(axis)
    return lax.ppermute(value, axis, [(i, i ^ bit) for i in range(n)])


def spread(value, axis):
    return (value + mix(value, axis, 1)) + (mix(value, axis, 2) + mix(value, axis, 3))


def tie(*values):
    return lax.optimization_barrier(values)


def onward(tail):
    return lax.ppermute(tail, FS, [(i, i + 1) for i in range(63)])


def moved(kept, own, tail):
    first = jnp.minimum(kept // 16 * 16, ROWS - 48)
    offset = kept - first
    window = pl.ds(pl.multiple_of(first, 16), 48)
    row = lax.broadcasted_iota(jnp.int32, (48, SPARE), 0)
    column = lax.broadcasted_iota(jnp.int32, (48, SPARE), 1)
    pick = (row == column + offset).astype(jnp.bfloat16)
    row = lax.broadcasted_iota(jnp.int32, (48, tail.shape[1]), 0)
    fresh = jnp.logical_and(row >= offset, row < offset + SPARE)
    new = jnp.dot(pick, tail, preferred_element_type=jnp.float32)
    return window, jnp.where(fresh, new, own[window, :].astype(jnp.float32)).astype(jnp.bfloat16)


def rows_kernel(where, own, tail, out_ref):
    out_ref[...] = own[...]
    window, new = moved(where[0], own, tail[...])
    out_ref[window, :] = new


def half_rows(where, rows, tail):
    return pl.pallas_call(
        rows_kernel,
        grid_spec=pltpu.PrefetchScalarGridSpec(
            num_scalar_prefetch=1,
            grid=(1,),
            in_specs=[
                pl.BlockSpec((ROWS, 2048), lambda i, where: (0, where[1])),
                pl.BlockSpec((SPARE, 2048), lambda i, where: (0, 0)),
            ],
            out_specs=pl.BlockSpec((ROWS, 2048), lambda i, where: (0, 0)),
        ),
        out_shape=jax.ShapeDtypeStruct((ROWS, 2048), jnp.bfloat16),
        compiler_params=pltpu.CompilerParams(vmem_limit_bytes=32 * MIB),
        name="rows",
    )(where, rows, tail)


def place_kernel(kept, gate, up, tails, gate_out, up_out):
    for own, tail, out in ((gate, tails[0], gate_out), (up, tails[1], up_out)):
        out[...] = own[...]
        window, new = moved(kept[0], own, tail)
        out[window, :] = new


def placed(kept, gate, up, tails):
    vmem = pl.BlockSpec(memory_space=pltpu.VMEM)
    return pl.pallas_call(
        place_kernel,
        in_specs=[pl.BlockSpec(memory_space=pltpu.SMEM)] + [vmem] * 3,
        out_specs=[vmem] * 2,
        out_shape=[jax.ShapeDtypeStruct((ROWS, MINE), jnp.bfloat16)] * 2,
        compiler_params=pltpu.CompilerParams(vmem_limit_bytes=60 * MIB),
        cost_estimate=pl.CostEstimate(flops=0, bytes_accessed=8 * ROWS * MINE, transcendentals=0),
        name="place",
    )(kept, gate, up, tails)


def start_all(pairs, sems):
    copies = [pltpu.make_async_copy(a, b, sems.at[k]) for k, (a, b) in enumerate(pairs)]
    for copy in copies:
        copy.start()
    return copies


def wait_all(copies):
    for copy in copies:
        copy.wait()


def probe_kernel(pos, rows_ref, *refs):
    parts, outs, (weight, rows, sems) = refs[:4], refs[4:8], refs[8:]
    waits = []
    for ky in range(4):
        half = pos[ky] // 2
        lanes = pl.ds(pl.multiple_of(lax.rem(pos[ky], 2) * 1024, 1024), 1024)
        pairs = [(parts[ky].at[k], weight.at[ky, :, pos[8 + k]]) for k in range(4)]
        for k in range(4):
            to = rows.at[ky, pl.ds(k * ROWS, ROWS)]
            pairs.append((rows_ref.at[pos[4 + k] * 2 + half, :, lanes], to))
        waits.append(start_all(pairs, sems.at[ky]))
    for ky in range(4):
        wait_all(waits[ky])
        product = jnp.dot(
            rows[ky], weight[ky].reshape(1024, -1), preferred_element_type=jnp.float32
        )
        for k in range(4):
            value = product[k * ROWS : (k + 1) * ROWS] * (1.0 / D**0.5)
            outs[k][...] = value if ky == 0 else outs[k][...] + value


def probes(pos, rows, parts):
    wide = parts[0].shape[-1]
    vmem = pl.BlockSpec(memory_space=pltpu.VMEM)
    return pl.pallas_call(
        probe_kernel,
        in_specs=[pl.BlockSpec(memory_space=pltpu.SMEM)] + [pl.BlockSpec(memory_space=pl.ANY)] * 5,
        out_specs=[vmem] * 4,
        scratch_shapes=[
            pltpu.VMEM((4, 4, 4, 64, wide), jnp.bfloat16),
            pltpu.VMEM((4, 4 * ROWS, 1024), jnp.bfloat16),
            pltpu.SemaphoreType.DMA((4, 8)),
        ],
        out_shape=[jax.ShapeDtypeStruct((ROWS, wide), jnp.float32)] * 4,
        compiler_params=pltpu.CompilerParams(vmem_limit_bytes=28 * MIB),
        cost_estimate=pl.CostEstimate(
            flops=8 * ROWS * D * wide, bytes_accessed=2 * D * (1024 + wide), transcendentals=0
        ),
        name="probe",
    )(pos, rows, *parts)


def tiles(pos):
    for k in range(4):
        member = pos[4 + k]
        for t in range(CHUNK // LANES):
            cut = max(i for i, (first, _) in enumerate(CUTS) if first <= t * LANES)
            there = t * LANES - CUTS[cut][0]
            place = pl.multiple_of(member * STEP + t * LANES, LANES)
            yield 4 * cut + k, slice(there, there + LANES), pl.ds(place, LANES), t, member


def score_kernel(pos, gate_ref, up_ref, *refs):
    pieces, out_ref = refs[:-1], refs[-1]
    acc = jnp.zeros((LANES, LANES), jnp.float32)
    for k, there, here, t, member in tiles(pos):
        gate = gate_ref[:, here].astype(jnp.float32)
        up = up_ref[:, here].astype(jnp.float32)
        term = gate * jax.nn.sigmoid(gate) * up * pieces[k][:, there]
        if t == CHUNK // LANES - 1:
            term = jnp.where(member == 3, term, 0.0)
        acc = acc + term
    out_ref[0] = jnp.sum(acc.T, axis=0, keepdims=True)


def piece_specs(rows):
    return [pl.BlockSpec((rows, n), lambda i, pos: (i, 0)) for _, n in CUTS for _ in range(4)]


def scores(pos, gate, up, pieces):
    wide = pl.BlockSpec((LANES, MINE), lambda i, pos: (i, 0))
    return pl.pallas_call(
        score_kernel,
        grid_spec=pltpu.PrefetchScalarGridSpec(
            num_scalar_prefetch=1,
            grid=(2,),
            in_specs=[wide, wide] + piece_specs(LANES),
            out_specs=pl.BlockSpec((1, 1, LANES), lambda i, pos: (i, 0, 0)),
        ),
        out_shape=jax.ShapeDtypeStruct((2, 1, LANES), jnp.float32),
        compiler_params=pltpu.CompilerParams(vmem_limit_bytes=40 * MIB),
        cost_estimate=pl.CostEstimate(
            flops=8 * ROWS * MINE, bytes_accessed=8 * ROWS * MINE, transcendentals=ROWS * MINE
        ),
        name="score",
    )(pos, gate, up, *pieces)


def info_kernel(nums, advs, old_ref, info_ref, tail_ref):
    at = lax.broadcasted_iota(jnp.int32, (1, ROWS), 1)
    in_first = at < nums[0]
    in_second = jnp.logical_and(at >= nums[0], at < nums[0] + nums[1])
    adv = jnp.where(in_first, advs[0], 0.0) + jnp.where(in_second, advs[1], 0.0)
    live = jnp.logical_or(in_first, in_second).astype(jnp.float32)
    row = lax.broadcasted_iota(jnp.int32, (8, ROWS), 0)
    info = jnp.where(row == 0, old_ref[...], jnp.where(row == 1, adv, live))
    info_ref[...] = info
    tail_ref[...] = pltpu.roll(info, ROWS - nums[2], 1)[:, :LANES]


def infos(nums, advs, old):
    smem = pl.BlockSpec(memory_space=pltpu.SMEM)
    return pl.pallas_call(
        info_kernel,
        in_specs=[smem, smem, pl.BlockSpec(memory_space=pltpu.VMEM)],
        out_shape=(
            jax.ShapeDtypeStruct((8, ROWS), jnp.float32),
            jax.ShapeDtypeStruct((8, LANES), jnp.float32),
        ),
        name="info",
    )(nums, advs, old)


def slope_kernel(nums, score_ref, info_ref, tail_ref, count_ref, slope_ref, loss_ref):
    at = lax.broadcasted_iota(jnp.int32, (8, ROWS), 1)
    fresh = jnp.logical_and(at >= nums[2], at < nums[2] + SPARE)
    tail = jnp.concatenate([tail_ref[...], tail_ref[...]], axis=1)
    info = jnp.where(fresh, pltpu.roll(tail, nums[2], 1), info_ref[...])
    loss = jnp.zeros((1, LANES), jnp.float32)
    for i in range(2):
        here = slice(i * LANES, (i + 1) * LANES)
        old, adv, mask = info[0:1, here], info[1:2, here], info[2:3, here]
        ratio = jnp.exp(score_ref[i] - old)
        plain = ratio * adv
        clipped = jnp.clip(ratio, 0.8, 1.2) * adv
        loss = loss + mask * jnp.minimum(plain, clipped)
        slope = jnp.where(plain <= clipped, -adv * ratio, 0.0) * mask / count_ref[...]
        slope_ref[here, :] = jnp.broadcast_to(slope, (LANES, LANES)).T
    loss_ref[...] = loss


def slopes(nums, score, info, tail, count):
    vmem = pl.BlockSpec(memory_space=pltpu.VMEM)
    return pl.pallas_call(
        slope_kernel,
        in_specs=[pl.BlockSpec(memory_space=pltpu.SMEM)] + [vmem] * 4,
        out_shape=(
            jax.ShapeDtypeStruct((ROWS, LANES), jnp.float32),
            jax.ShapeDtypeStruct((1, LANES), jnp.float32),
        ),
        name="slope",
    )(nums, score, info, tail, count)


def grad_kernel(pos, gate_ref, up_ref, slope_ref, *refs):
    pieces, (gate_out, up_out) = refs[:-2], refs[-2:]
    slope = slope_ref[...]
    for k, there, here, _, _ in tiles(pos):
        gate = gate_ref[:, here].astype(jnp.float32)
        up = up_ref[:, here].astype(jnp.float32)
        sig = jax.nn.sigmoid(gate)
        dhidden = slope * pieces[k][:, there]
        gate_out[:, here] = (dhidden * up * sig * (1.0 + gate * (1.0 - sig))).astype(jnp.bfloat16)
        up_out[:, here] = (dhidden * (gate * sig)).astype(jnp.bfloat16)


def grads(pos, gate, up, slope, pieces):
    rows = 64
    wide = pl.BlockSpec((rows, MINE), lambda i, pos: (i, 0))
    return pl.pallas_call(
        grad_kernel,
        grid_spec=pltpu.PrefetchScalarGridSpec(
            num_scalar_prefetch=1,
            grid=(ROWS // rows,),
            in_specs=[wide, wide, pl.BlockSpec((rows, LANES), lambda i, pos: (i, 0))]
            + piece_specs(rows),
            out_specs=[wide, wide],
        ),
        out_shape=[jax.ShapeDtypeStruct((ROWS, MINE), jnp.bfloat16)] * 2,
        compiler_params=pltpu.CompilerParams(vmem_limit_bytes=60 * MIB),
        cost_estimate=pl.CostEstimate(
            flops=12 * ROWS * MINE, bytes_accessed=12 * ROWS * MINE, transcendentals=ROWS * MINE
        ),
        name="grad",
    )(pos, gate, up, slope, *pieces)


def shards(gate_pre, up_pre, target_rows, down_weight, old_logp, advantages, lengths, handoff):
    at = {a: lax.axis_index(a) for a in ("y", "x", "h", "c")}
    ahead = [0, 1 + 2 * at["c"], 3 + 2 * at["c"], 2]
    behind = [0, 3 + 2 * at["c"], 1 + 2 * at["c"], 2]
    to_x = [lax.rem(at["x"] + k, 4) for k in ahead]
    from_x = [lax.rem(at["x"] + k, 4) for k in behind]
    kept = lengths[0] + lengths[1] - handoff[0]
    columns = down_weight.T
    chunks = [lax.dynamic_slice_in_dim(columns, x * STEP, CHUNK, 1) for x in to_x]
    chunks, target_rows, kept, lengths = tie(chunks, target_rows, kept, lengths)
    sent = [chunks[0]] + [swing(chunks[way], "x", way) for way in (SIDE, OTHER, FAR)]
    sent, target_rows, lengths, kept = tie(sent, target_rows, lengths, kept)
    tail = onward(lax.dynamic_slice(target_rows, (kept, at["c"] * 2048), (SPARE, 2048)))
    nums = jnp.stack([lengths[0], lengths[1], kept]).astype(jnp.int32)
    info, info_tail = infos(nums, advantages, old_logp.reshape(1, ROWS))
    info_tail = onward(info_tail)
    count = jnp.full((1, LANES), jnp.sum(lengths).astype(jnp.float32))
    mine = []
    for x in range(4):
        piece = sent[0]
        for k in (SIDE, OTHER, FAR):
            piece = jnp.where(from_x[k] == x, sent[k], piece)
        mine.append(piece)
    pos = [lax.rem(at["y"] + k, 4) for k in behind] + from_x
    pos = jnp.stack(pos + [lax.rem(at["h"] + k, 4) for k in behind]).astype(jnp.int32)

    block = jnp.stack(mine)
    block = [block[:, :, a : a + n] for a, n in CUTS]
    tails = jnp.stack([lax.dynamic_slice_in_dim(a, kept, SPARE, 0) for a in (gate_pre, up_pre)])

    def there(value, axis):
        return swing(value, axis, SIDE), swing(value, axis, OTHER)

    def again(side, axis):
        return swing(side, axis, SIDE)

    def returned(product):
        home = [product[OWN], None, None, None]
        for k, way in ((SIDE, OTHER), (OTHER, SIDE), (FAR, FAR)):
            home[way] = swing(product[k], "x", way)
        return home

    side, other = there(block[0], "h")
    side, other, tail = tie(side, other, tail)
    far = again(side, "h")
    where = jnp.stack([kept, at["c"]]).astype(jnp.int32)
    group = lax.all_gather(half_rows(where, target_rows, tail), ("x", "c"), axis=0)
    home, parts = [], None
    last = len(CUTS) - 1
    for i in range(last + 1):
        wide = jnp.stack([block[i], side, other, far])
        wide, block, parts, count = tie(wide, block, parts, count)
        a, b = there(wide, "y")
        if i < last:
            side, other = there(block[i + 1], "h")
        if i == 0:
            count = lax.psum(count, "x")
        product = probes(pos, group, parts) if i else None
        a, b, side, other, count, product, home, tails, info_tail = tie(
            a, b, side, other, count, product, home, tails, info_tail
        )
        if i:
            home = home + returned(product)
        c = again(a, "y")
        if i < last:
            far = again(side, "h")
        if i == last - 1:
            count = lax.psum(count, "h")
        parts = [wide, a, b, c]
    tails = onward(tails)
    product = probes(pos, group, parts)
    product, home, count, tails = tie(product, home, count, tails)
    home = home + returned(product)
    count = lax.psum(count, "y")
    gate, up = placed(kept.reshape(1).astype(jnp.int32), gate_pre, up_pre, tails)
    gate, up, count, home[-3], home[-2] = tie(gate, up, count, home[-3], home[-2])
    score = lax.psum(scores(pos, gate, up, home), ("l", "c"))
    slope, loss_part = slopes(nums, score, info, info_tail, count)
    loss_part = spread(loss_part, "h")
    gate_grad, up_grad = grads(pos, gate, up, slope, home)
    loss_part, gate_grad, up_grad = tie(loss_part, gate_grad, up_grad)
    loss_sum = jnp.sum(spread(spread(loss_part, "y"), "x"))
    return gate_grad, up_grad, -loss_sum / count[0, 0]


def solution(mesh):
    grid = Mesh(mesh.devices.reshape(4, 4, 4, 2, 2), ("y", "x", "h", "l", "c"))
    sp = ("l", "c")
    return jax.shard_map(
        shards,
        mesh=grid,
        in_specs=(P(FS, sp), P(FS, sp), P(FS, None), P(sp, FS), P(FS), P(FS), P(FS), P(FS)),
        out_specs=(P(FS, sp), P(FS, sp), P()),
        check_vma=False,
    )
```
